32 devices in a mesh: grp: 4 (over y, core), ctx: 8 (over z, x).
Axes of the slice: x: 2, y: 2, z: 4, core: 2. Of those that a mesh axis runs over, the one named last changes fastest.
Arguments:
- query_rows: bfloat16 [4, 1024, 4096], P('grp', 'ctx'), may hold values from -6 to 6
- key_rows: bfloat16 [4, 1024, 512], P('grp', 'ctx'), may hold values from -6 to 6
- value_rows: bfloat16 [4, 1024, 512], P('grp', 'ctx'), may hold values from -5 to 5
- output_rows: bfloat16 [4, 1024, 4096], P('grp', 'ctx'), may hold values from -4 to 4
- output_grad: bfloat16 [4, 1024, 4096], P('grp', 'ctx'), may hold values from -5 to 5
- loss_mask: int32 [4, 1024], P('grp', 'ctx'), may hold values from 0 to 1
- doc_lengths: int32 [4, 12], P('grp'), may hold values from 1 to 256, 1024 in all within a row
- balance_plan: int32 [4, 128], P('grp'), may hold values from 0 to 127, as said below
Outputs:
- query_grad: bfloat16 [4, 1024, 4096], P('grp', 'ctx')
- key_grad: bfloat16 [4, 1024, 512], P('grp', 'ctx')
- value_grad: bfloat16 [4, 1024, 512], P('grp', 'ctx')
The draws below stay inside these ranges and needn't reach their ends.
Inputs may be any that keep to these rules, and one draw needn't show every extreme that they name: Each row is a permutation of 0 to 127. Span c of a sequence (its tokens c * 8 to c * 8 + 7) goes to index balance_plan // 16 of ctx; of the 16 spans of one index of ctx at most 2 go to the same index.
All inputs are finite; a program needn't handle non-finite values.
Results may differ from the reference program's by a relative error of at most 0.0051.
Values may be sent and summed in bfloat16 or wider, within the bound.
A program may use at most 128 MiB of HBM per device.

```python
import math
import jax
import jax.numpy as jnp
import numpy as np
from jax import lax

HD = 128
QH = 32
KVH = 4
SPAN = 8
DOCS = 12
SEQS = 4
SEQ_LEN = 1024
SPANS_DEV = 16
SPANS = 128


def draw_query_rows(key, part):
    row_width = QH * HD
    result = jnp.clip(jax.random.normal(jax.random.fold_in(key, 1), (SEQS, SEQ_LEN, row_width), jnp.float32), -5.0, 5.0)
    return result.astype(jnp.bfloat16)


def draw_key_rows(key, part):
    row_width = KVH * HD
    result = jnp.clip(jax.random.normal(jax.random.fold_in(key, 2), (SEQS, SEQ_LEN, row_width), jnp.float32), -5.0, 5.0)
    return result.astype(jnp.bfloat16)


def draw_loss_mask(key, part):
    positions = jnp.arange(SEQ_LEN, dtype=jnp.int32)
    threshold = 250 + 500 * positions // SEQ_LEN
    drawn = jax.random.randint(key, (SEQS, SEQ_LEN), 0, 1000)
    return (drawn < threshold[None, :]).astype(jnp.int32)


def draw_balance_plan(key, part):
    per_device = SPANS_DEV
    devices = SPANS // SPANS_DEV
    replicas = (per_device + devices - 1) // devices

    def one_sequence(seq_key):
        offsets = jnp.concatenate([jax.random.permutation(jax.random.fold_in(seq_key, replica), devices) for replica in range(replicas)])[:per_device]
        orders = jax.vmap(lambda source: jax.random.permutation(jax.random.fold_in(seq_key, 1000 + source), per_device))(jnp.arange(devices))
        sources = jnp.arange(devices, dtype=jnp.int32)[:, None]
        target = (sources + offsets[orders]) % devices
        return (target * per_device + orders).reshape(-1).astype(jnp.int32)
    return jax.vmap(lambda seq_number: one_sequence(jax.random.fold_in(key, seq_number)))(jnp.arange(SEQS))


def levels(key, shape, cuts, smallest, top_value):
    level, own = 1.0, jax.random.fold_in(key, 6)
    for dim, parts in cuts:
        steps = jnp.exp(jax.random.uniform(jax.random.fold_in(own, dim), (parts,), jnp.float32, smallest / len(cuts), top_value / len(cuts)))
        level = level * jnp.repeat(steps, shape[dim] // parts).reshape([-1 if axis == dim else 1 for axis in range(len(shape))])
    return level


def profile(amount, total, reach, lean):
    weights = [(1 << 20) // math.isqrt(rank ** lean) + 1 for rank in range(2, amount + 1)]
    surplus, holding = total - reach - (amount - 1), [1] * (amount - 1)
    while surplus > 0:
        candidates = [i for i in range(amount - 1) if holding[i] < reach]
        pool, remaining = sum([weights[i] for i in candidates]), surplus
        for i in candidates:
            more = min(reach - holding[i], max(1, remaining * weights[i] // pool), surplus)
            holding[i] = holding[i] + more
            surplus = surplus - more
    return np.array([reach] + holding)


def uneven(stream_key, number_of, total, most, slope):
    if number_of == 2:
        one = jax.random.randint(stream_key, (), max(1, total - most), min(most, total - 1) + 1)
        return jnp.stack([one, total - one])
    lengths = jnp.asarray(profile(number_of, total, most, slope), jnp.int32)
    twos = (number_of - 1) // 2
    donor, receiver = lengths[1:1 + 2 * twos:2], lengths[2:2 + 2 * twos:2]
    margin = jnp.minimum(donor - 1, most - receiver)
    passed = jax.random.randint(jax.random.fold_in(stream_key, 1), (twos,), 0, 1 << 20) % (margin + 1)
    lengths = lengths.at[1:1 + 2 * twos:2].set(donor - passed).at[2:2 + 2 * twos:2].set(receiver + passed)
    return lengths[jax.random.permutation(jax.random.fold_in(stream_key, 2), number_of)]


def gaussian(key, dims, width, limit, pieces=(), kind=jnp.bfloat16):
    level = levels(key, dims, pieces, -0.22, 0.18) if pieces else 1.0
    values = jax.random.normal(key, dims, jnp.float32) * width * level
    return jnp.minimum(jnp.maximum(values, -limit), limit).astype(kind)


def setup_inputs(seed: int = 0) -> dict:
    arg_keys = jax.random.split(jax.random.key(seed), 9)
    return {
        "query_rows": draw_query_rows(jax.random.fold_in(arg_keys[8], 71), 0),
        "key_rows": draw_key_rows(jax.random.fold_in(arg_keys[8], 71), 0),
        "value_rows": gaussian(arg_keys[2], (SEQS, SEQ_LEN, KVH * HD), 1.0, 5.0, ((0, 4), (1, 8))),
        "output_rows": gaussian(arg_keys[3], (SEQS, SEQ_LEN, QH * HD), 0.5, 4.0, ((0, 4), (1, 8))),
        "output_grad": gaussian(arg_keys[4], (SEQS, SEQ_LEN, QH * HD), 1.0, 5.0, ((0, 4), (1, 8))),
        "loss_mask": draw_loss_mask(jax.random.fold_in(arg_keys[8], 71), 0),
        "doc_lengths": jax.vmap(lambda own: uneven(own, DOCS, SEQ_LEN, SEQ_LEN // 4, 2))(jax.random.split(arg_keys[6], SEQS)).reshape((SEQS, DOCS)).astype(jnp.int32),
        "balance_plan": draw_balance_plan(jax.random.fold_in(arg_keys[8], 71), 0),
    }


NEGATIVE = -1.0e30


def doc_index(positions, doc_ends):
    return jnp.sum((positions[:, None] >= doc_ends[None, :]).astype(jnp.int32), axis=1)


def sequence_grads(query_seq, key_seq, value_seq, output_seq, grad_seq, lengths_seq):
    seq_total = query_seq.shape[0]
    block_rows = 512 if seq_total % 512 == 0 else seq_total
    block_count = seq_total // block_rows
    group_size = QH // KVH
    scale_value = HD ** -0.5
    doc_ends = jnp.cumsum(lengths_seq)
    key_pos = jnp.arange(seq_total, dtype=jnp.int32)
    key_doc = doc_index(key_pos, doc_ends)
    k_heads = key_seq.astype(jnp.float32).reshape(seq_total, KVH, HD)
    v_heads = value_seq.astype(jnp.float32).reshape(seq_total, KVH, HD)
    q_blocks = query_seq.reshape(block_count, block_rows, KVH, group_size, HD)
    g_blocks = grad_seq.reshape(block_count, block_rows, KVH, group_size, HD)
    o_blocks = output_seq.reshape(block_count, block_rows, KVH, group_size, HD)

    def one_block(carried, scanned):
        block_index, q_block, g_block, o_block = scanned
        query_pos = block_index * block_rows + jnp.arange(block_rows, dtype=jnp.int32)
        query_doc = doc_index(query_pos, doc_ends)
        visible_mask = (key_pos[None, :] <= query_pos[:, None]) & (key_doc[None, :] == query_doc[:, None])
        q_float = q_block.astype(jnp.float32)
        g_float = g_block.astype(jnp.float32)
        scores = jnp.einsum("rgsd,ngd->gsrn", q_float, k_heads) * scale_value
        masked = jnp.where(visible_mask, scores, NEGATIVE)
        row_peak = jnp.max(masked, axis=-1)
        row_sum = jnp.sum(jnp.where(visible_mask, jnp.exp(masked - row_peak[..., None]), 0.0), axis=-1)
        lse_rows = row_peak + jnp.log(row_sum)
        probs_full = jnp.where(visible_mask, jnp.exp(jnp.where(visible_mask, scores - lse_rows[..., None], NEGATIVE)), 0.0)
        probs_half = lax.optimization_barrier(probs_full.astype(jnp.bfloat16)).astype(jnp.float32)
        delta_rows = jnp.transpose(jnp.sum(g_float * o_block.astype(jnp.float32), axis=-1), (1, 2, 0))
        dprobs = jnp.einsum("rgsd,ngd->gsrn", g_float, v_heads)
        dscores = (probs_full * (dprobs - delta_rows[..., None]) * scale_value).astype(jnp.bfloat16)
        dscores = lax.optimization_barrier(dscores).astype(jnp.float32)
        dq_block = jnp.einsum("gsrn,ngd->rgsd", dscores, k_heads)
        dk_sum = carried[0] + jnp.einsum("gsrn,rgsd->ngd", dscores, q_float)
        dv_sum = carried[1] + jnp.einsum("gsrn,rgsd->ngd", probs_half, g_float)
        return (dk_sum, dv_sum), dq_block

    initial = (jnp.zeros((seq_total, KVH, HD), jnp.float32), jnp.zeros((seq_total, KVH, HD), jnp.float32))
    scanned_in = (jnp.arange(block_count, dtype=jnp.int32), q_blocks, g_blocks, o_blocks)
    (dk_total, dv_total), dq_blocks = lax.scan(one_block, initial, scanned_in)
    return dq_blocks.reshape(seq_total, QH * HD), dk_total, dv_total


def reference(query_rows, key_rows, value_rows, output_rows, output_grad, loss_mask, doc_lengths, balance_plan):
    counted = jnp.sum(loss_mask.astype(jnp.float32))
    factor = (SEQS * SEQ_LEN) / jnp.maximum(counted, 1.0)
    grad_masked = output_grad * loss_mask[:, :, None].astype(jnp.bfloat16)
    query_list = []
    key_list = []
    value_list = []
    for seq_index in range(query_rows.shape[0]):
        dq_seq, dk_seq, dv_seq = sequence_grads(query_rows[seq_index], key_rows[seq_index], value_rows[seq_index], output_rows[seq_index], grad_masked[seq_index], doc_lengths[seq_index])
        inverse = jnp.argsort(balance_plan[seq_index]).astype(jnp.int32)
        dq_spans = (dq_seq * factor).astype(jnp.bfloat16).reshape(SPANS, SPAN, QH * HD)
        query_list.append(jnp.take(dq_spans, inverse, axis=0).reshape(SEQ_LEN, QH * HD))
        key_list.append((dk_seq * factor).astype(jnp.bfloat16).reshape(SEQ_LEN, KVH * HD))
        value_list.append((dv_seq * factor).astype(jnp.bfloat16).reshape(SEQ_LEN, KVH * HD))
    return (jnp.stack(query_list), jnp.stack(key_list), jnp.stack(value_list))
```

```python
import functools
import math

import jax
import jax.numpy as jnp
from jax import lax
from jax.experimental import pallas as pl
from jax.experimental.pallas import tpu as pltpu
from jax.sharding import PartitionSpec as P

HD = 128
QH = 32
KVH = 4
SPAN = 8
GROUP = QH // KVH
NEGATIVE = -1e30
MESH = pl.DeviceIdType.MESH


def dot(a, b, ca, cb):
    return lax.dot_general(a, b, (((ca,), (cb,)), ((), ())), preferred_element_type=jnp.float32)


def kernel(
    n, grps, halo, pair_rows,
    q_ref, k_ref, v_ref, o_ref, g_ref, mask_ref, docs_ref, plan_ref,
    dq_ref, dk_ref, dv_ref,
    kvwin, part_send, part_recv, part_own, dq_send, dq_recv, cnt_ctx, cnt_grp, bias_ref,
    kv_ss, kv_rs, pt_ss, pt_rs, dq_ss, dq_rs, c1_ss, c1_rs, c2_ss, c2_rs,
):
    me = lax.axis_index("ctx")
    my_grp = lax.axis_index("grp")
    rows = q_ref.shape[1]
    spans = plan_ref.shape[1]
    per_device = rows // SPAN
    slots = halo + 1
    window = slots * rows
    width = GROUP * HD
    peers = [lax.rem(me + step, n) for step in range(1, n)]
    grp_peers = [lax.rem(my_grp + step, grps) for step in range(1, grps)]

    barrier = pltpu.get_barrier_semaphore()
    for peer in peers:
        pl.semaphore_signal(barrier, inc=1, device_id={"ctx": peer}, device_id_type=MESH)
    for peer in grp_peers:
        pl.semaphore_signal(barrier, inc=1, device_id={"grp": peer}, device_id_type=MESH)

    for g in range(KVH):
        kvwin[g, 0, halo] = k_ref[0, :, g * HD:(g + 1) * HD]
        kvwin[g, 1, halo] = v_ref[0, :, g * HD:(g + 1) * HD]
    mask_f = mask_ref[...].astype(jnp.float32)
    cnt_ctx[me] = jnp.broadcast_to(jnp.sum(mask_f, axis=1, keepdims=True), (8, 128))

    pl.semaphore_wait(barrier, n - 1 + grps - 1)

    def kv_copy(g, s, target):
        return pltpu.make_async_remote_copy(
            src_ref=kvwin.at[g, :, halo], dst_ref=kvwin.at[g, :, halo - s],
            send_sem=kv_ss.at[g, s - 1], recv_sem=kv_rs.at[g, s - 1],
            device_id={"ctx": target}, device_id_type=MESH)

    def part_copy(g, s, target):
        return pltpu.make_async_remote_copy(
            src_ref=part_send.at[g, s - 1], dst_ref=part_recv.at[g, s - 1],
            send_sem=pt_ss.at[g, s - 1], recv_sem=pt_rs.at[g, s - 1],
            device_id={"ctx": target}, device_id_type=MESH)

    def dq_out(g, peer):
        return pltpu.make_async_remote_copy(
            src_ref=dq_send.at[g, peer], dst_ref=dq_recv.at[g, me],
            send_sem=dq_ss.at[g, peer], recv_sem=dq_rs.at[g, me],
            device_id={"ctx": peer}, device_id_type=MESH)

    def dq_in(g, peer):
        return pltpu.make_async_remote_copy(
            src_ref=dq_send.at[g, peer], dst_ref=dq_recv.at[g, peer],
            send_sem=dq_ss.at[g, peer], recv_sem=dq_rs.at[g, peer],
            device_id={"ctx": peer}, device_id_type=MESH)

    def count_copy(buffer, ss, rs, axis, own, slot, peer):
        return pltpu.make_async_remote_copy(
            src_ref=buffer.at[own], dst_ref=buffer.at[slot],
            send_sem=ss.at[peer], recv_sem=rs.at[slot],
            device_id={axis: peer}, device_id_type=MESH)

    for peer in peers:
        count_copy(cnt_ctx, c1_ss, c1_rs, "ctx", me, me, peer).start()
    for g in range(KVH):
        for s in range(1, halo + 1):
            @pl.when(me + s < n)
            def _():
                kv_copy(g, s, me + s).start()

    plan_f = plan_ref[...].astype(jnp.float32)
    plan_b = jnp.broadcast_to(plan_f, (spans, spans))
    plan_t = jnp.transpose(plan_b)
    dest_b = jnp.floor(plan_b * (1.0 / per_device))
    dest_t = jnp.floor(plan_t * (1.0 / per_device))
    row_id = lax.broadcasted_iota(jnp.int32, (spans, spans), 0)
    col_id = lax.broadcasted_iota(jnp.int32, (spans, spans), 1)
    earlier = (dest_b == dest_t) & (row_id // per_device == col_id // per_device) & (col_id < row_id)
    rank_t = jnp.sum(jnp.where(earlier, 1.0, 0.0), axis=1, keepdims=True)
    span_id = lax.broadcasted_iota(jnp.int32, (spans, rows), 0)
    tok_id = lax.broadcasted_iota(jnp.int32, (spans, rows), 1)
    dest_c = dest_t[:, :1]
    plan_c = plan_t[:, :1]
    send_c = dest_c * float(pair_rows) + rank_t * float(SPAN)
    origin = (lax.broadcasted_iota(jnp.int32, (spans, 1), 0) // per_device).astype(jnp.float32)
    recv_c = origin * float(pair_rows) + rank_t * float(SPAN)
    tok = lax.broadcasted_iota(jnp.int32, (1, rows), 1)
    within = lax.rem(tok, SPAN).astype(jnp.float32)
    own_span = span_id == me * per_device + tok_id // SPAN
    send_row = jnp.sum(jnp.where(own_span, send_c, 0.0), axis=0, keepdims=True) + within
    slot_f = (me * per_device + tok_id // SPAN).astype(jnp.float32)
    recv_row = jnp.sum(jnp.where(plan_c == slot_f, recv_c, 0.0), axis=0, keepdims=True) + within
    buffer_id = lax.broadcasted_iota(jnp.int32, (n * pair_rows, rows), 0).astype(jnp.float32)
    pack = jnp.where(buffer_id == send_row, 1.0, 0.0).astype(jnp.bfloat16)
    unpack = jnp.transpose(jnp.where(buffer_id == recv_row, 1.0, 0.0)).astype(jnp.bfloat16)

    query_pos = me * rows + tok
    start = jnp.zeros_like(query_pos)
    end = jnp.int32(0)
    for m in range(docs_ref.shape[1]):
        end = end + docs_ref[0, m]
        start = jnp.where(query_pos >= end, end, start)
    key_pos = (me - halo) * rows + lax.broadcasted_iota(jnp.int32, (window, rows), 0)
    bias_ref[...] = jnp.where((key_pos >= start) & (key_pos <= query_pos), 0.0, NEGATIVE)
    mask_col = jnp.transpose(jnp.broadcast_to(mask_f, (HD, rows))).astype(jnp.bfloat16)

    for peer in peers:
        count_copy(cnt_ctx, c1_ss, c1_rs, "ctx", me, peer, peer).wait_recv()
    cnt_grp[my_grp] = jnp.sum(cnt_ctx[...], axis=0)
    for peer in grp_peers:
        count_copy(cnt_grp, c2_ss, c2_rs, "grp", my_grp, my_grp, peer).start()

    scale_value = HD ** (-0.5)
    exp_scale = scale_value * math.log2(math.e)
    ones = jnp.ones((8, 2 * HD), jnp.bfloat16)
    factor = None
    for g in range(KVH):
        for s in range(1, halo + 1):
            @pl.when(me >= s)
            def _():
                kv_copy(g, s, me).wait_recv()

            @pl.when(me < s)
            def _():
                kvwin[g, :, halo - s] = jnp.zeros((2, rows, HD), jnp.bfloat16)
        keys = kvwin[g, 0].reshape(window, HD)
        values = kvwin[g, 1].reshape(window, HD)
        keys_t = jnp.transpose(keys)
        dk_sum = jnp.zeros((window, HD), jnp.float32)
        dv_sum = jnp.zeros((window, HD), jnp.float32)
        for pair in range(GROUP // 2):
            columns = [slice(h * HD, (h + 1) * HD) for h in (g * GROUP + 2 * pair, g * GROUP + 2 * pair + 1)]
            queries = jnp.concatenate([q_ref[0, :, c] for c in columns], axis=0)
            grads = jnp.concatenate([g_ref[0, :, c] * mask_col for c in columns], axis=0)
            outputs = jnp.concatenate([o_ref[0, :, c] for c in columns], axis=0)
            product = grads.astype(jnp.float32) * outputs.astype(jnp.float32)
            high = product.astype(jnp.bfloat16)
            low = (product - high.astype(jnp.float32)).astype(jnp.bfloat16)
            delta = dot(ones, jnp.concatenate([high, low], axis=1), 1, 1)[:1]
            bias = bias_ref[...]
            scores = dot(keys, queries, 1, 1) * exp_scale + jnp.concatenate([bias, bias], axis=1)
            weights = jnp.exp2(scores - jnp.max(scores, axis=0, keepdims=True))
            probs = weights * (1.0 / jnp.sum(weights, axis=0, keepdims=True))
            dprobs = dot(values, grads, 1, 1)
            dscores = (probs * (dprobs - delta) * scale_value).astype(jnp.bfloat16)
            dq_t = dot(keys_t, dscores, 1, 0)
            if factor is None:
                for peer in grp_peers:
                    count_copy(cnt_grp, c2_ss, c2_rs, "grp", my_grp, peer, peer).wait_recv()
                counted = jnp.sum(cnt_grp[...], axis=0)[:1, :]
                factor = float(grps * n * rows) / jnp.maximum(counted, 1.0)
            dq_half = (dq_t * factor[:, :1]).astype(jnp.bfloat16)
            for i in range(2):
                packed = dot(pack, dq_half[:, i * rows:(i + 1) * rows], 1, 1).astype(jnp.bfloat16)
                local = (2 * pair + i) * HD
                dq_send[g, :, :, local:local + HD] = packed.reshape(n, pair_rows, HD)
            dk_sum += dot(dscores, queries, 1, 0)
            dv_sum += dot(probs.astype(jnp.bfloat16), grads, 1, 0)
        for peer in peers:
            dq_out(g, peer).start()
        dq_recv[g, me] = dq_send[g, me]
        for s in range(1, halo + 1):
            at = slice((halo - s) * rows, (halo - s + 1) * rows)
            part_send[g, s - 1, 0] = dk_sum[at].astype(jnp.bfloat16)
            part_send[g, s - 1, 1] = dv_sum[at].astype(jnp.bfloat16)

            @pl.when(me >= s)
            def _():
                part_copy(g, s, me - s).start()
        part_own[g, 0] = dk_sum[halo * rows:]
        part_own[g, 1] = dv_sum[halo * rows:]

    for g in range(KVH):
        for s in range(1, halo + 1):
            @pl.when(me + s < n)
            def _():
                part_copy(g, s, me).wait_recv()

            @pl.when(me + s >= n)
            def _():
                part_recv[g, s - 1] = jnp.zeros((2, rows, HD), jnp.bfloat16)
        total = part_own[g]
        for s in range(1, halo + 1):
            total += part_recv[g, s - 1].astype(jnp.float32)
        total = (total * factor[:, :1]).astype(jnp.bfloat16)
        dk_ref[0, :, g * HD:(g + 1) * HD] = total[0]
        dv_ref[0, :, g * HD:(g + 1) * HD] = total[1]
        for peer in peers:
            dq_in(g, peer).wait_recv()
        dq_ref[0, :, g * width:(g + 1) * width] = dot(
            unpack, dq_recv[g].reshape(n * pair_rows, width), 1, 0).astype(jnp.bfloat16)

    for peer in peers:
        count_copy(cnt_ctx, c1_ss, c1_rs, "ctx", me, me, peer).wait_send()
    for peer in grp_peers:
        count_copy(cnt_grp, c2_ss, c2_rs, "grp", my_grp, my_grp, peer).wait_send()
    for g in range(KVH):
        for s in range(1, halo + 1):
            @pl.when(me + s < n)
            def _():
                kv_copy(g, s, me + s).wait_send()

            @pl.when(me >= s)
            def _():
                part_copy(g, s, me - s).wait_send()
        for peer in peers:
            dq_out(g, peer).wait_send()


def solution(mesh):
    n, grps = mesh.shape["ctx"], mesh.shape["grp"]

    def shards(*args):
        rows = args[0].shape[1]
        halo = min(n - 1, -(-(n * rows // 4 - 1) // rows))
        slot_count = -(-(rows // SPAN) // n)
        pair_rows = -(-slot_count * SPAN // 16) * 16
        vmem = pl.BlockSpec(memory_space=pltpu.VMEM)
        smem = pl.BlockSpec(memory_space=pltpu.SMEM)
        dma = pltpu.SemaphoreType.DMA
        bf16, f32 = jnp.bfloat16, jnp.float32
        return pl.pallas_call(
            functools.partial(kernel, n, grps, halo, pair_rows),
            out_shape=[
                jax.ShapeDtypeStruct((1, rows, QH * HD), bf16),
                jax.ShapeDtypeStruct((1, rows, KVH * HD), bf16),
                jax.ShapeDtypeStruct((1, rows, KVH * HD), bf16),
            ],
            in_specs=[vmem] * 6 + [smem, vmem],
            out_specs=[vmem] * 3,
            scratch_shapes=[
                pltpu.VMEM((KVH, 2, halo + 1, rows, HD), bf16),
                pltpu.VMEM((KVH, halo, 2, rows, HD), bf16),
                pltpu.VMEM((KVH, halo, 2, rows, HD), bf16),
                pltpu.VMEM((KVH, 2, rows, HD), f32),
                pltpu.VMEM((KVH, n, pair_rows, GROUP * HD), bf16),
                pltpu.VMEM((KVH, n, pair_rows, GROUP * HD), bf16),
                pltpu.VMEM((n, 8, 128), f32),
                pltpu.VMEM((grps, 8, 128), f32),
                pltpu.VMEM(((halo + 1) * rows, rows), f32),
                dma((KVH, halo)), dma((KVH, halo)),
                dma((KVH, halo)), dma((KVH, halo)),
                dma((KVH, n)), dma((KVH, n)),
                dma((n,)), dma((n,)), dma((grps,)), dma((grps,)),
            ],
            compiler_params=pltpu.CompilerParams(
                collective_id=0, has_side_effects=True, vmem_limit_bytes=48 * 1024 * 1024),
            cost_estimate=pl.CostEstimate(
                flops=10 * (halo + 1) * rows * rows * QH * HD, bytes_accessed=9 * rows * QH * HD,
                transcendentals=(halo + 1) * rows * rows * QH),
        )(*args)

    in_specs = (
        P("grp", "ctx", None),
        P("grp", "ctx", None),
        P("grp", "ctx", None),
        P("grp", "ctx", None),
        P("grp", "ctx", None),
        P("grp", "ctx"),
        P("grp", None),
        P("grp", None),
    )
    out_specs = (P("grp", "ctx", None), P("grp", "ctx", None), P("grp", "ctx", None))
    return jax.shard_map(shards, mesh=mesh, in_specs=in_specs, out_specs=out_specs, check_vma=False)
```

```python
import functools
import math

import jax
import jax.numpy as jnp
from jax import lax
from jax.experimental import pallas as pl
from jax.experimental.pallas import tpu as pltpu
from jax.sharding import PartitionSpec as P

HD = 128
QH = 32
KVH = 4
SPAN = 8
GROUP = QH // KVH
NEGATIVE = -1e30
MESH = pl.DeviceIdType.MESH


def dot(a, b, ca, cb):
    return lax.dot_general(a, b, (((ca,), (cb,)), ((), ())), preferred_element_type=jnp.float32)


def kernel(
    n, grps, halo, pair_rows,
    q_hbm, k_hbm, v_hbm, o_hbm, g_hbm, mask_hbm, docs_hbm, plan_hbm,
    dq_ref, dk_ref, dv_ref,
    kvwin, part_send, part_recv, part_own, dq_send, dq_recv, cnt_ctx, cnt_grp, bias_ref,
    q_ref, o_ref, g_ref, mask_ref, docs_ref, plan_ref, kv_in, qog_in, small_in,
    kv_ss, kv_rs, pt_ss, pt_rs, dq_ss, dq_rs, c1_ss, c1_rs, c2_ss, c2_rs,
):
    me = lax.axis_index("ctx")
    my_grp = lax.axis_index("grp")
    rows = q_ref.shape[0]
    spans = plan_ref.shape[1]
    per_device = rows // SPAN
    slots = halo + 1
    window = slots * rows
    width = GROUP * HD
    steps = sorted(range(1, n), key=lambda step: (abs(2 * step - n), step))
    peers = [lax.rem(me + step, n) for step in steps]
    grp_peers = [lax.rem(my_grp + step, grps) for step in range(1, grps)]

    def fetch(source, target, sem):
        copy = pltpu.make_async_copy(source, target, sem)
        copy.start()
        return copy

    mask_copy = fetch(mask_hbm, mask_ref, small_in.at[0])
    kv_copies = [
        [fetch(ref.at[0, :, g * HD:(g + 1) * HD], kvwin.at[g, i, halo], kv_in.at[g, i])
         for i, ref in enumerate((k_hbm, v_hbm))]
        for g in range(KVH)
    ]
    plan_copy = fetch(plan_hbm, plan_ref, small_in.at[1])
    docs_copy = fetch(docs_hbm, docs_ref, small_in.at[2])
    qog_copies = [
        [fetch(source.at[0, :, g * width:(g + 1) * width], target.at[:, g * width:(g + 1) * width], qog_in.at[g, i])
         for i, (source, target) in enumerate(((q_hbm, q_ref), (o_hbm, o_ref), (g_hbm, g_ref)))]
        for g in range(KVH)
    ]

    barrier = pltpu.get_barrier_semaphore()
    for peer in peers:
        pl.semaphore_signal(barrier, inc=1, device_id={"ctx": peer}, device_id_type=MESH)
    for peer in grp_peers:
        pl.semaphore_signal(barrier, inc=1, device_id={"grp": peer}, device_id_type=MESH)

    mask_copy.wait()
    mask_f = mask_ref[...].astype(jnp.float32)
    cnt_ctx[me] = jnp.broadcast_to(jnp.sum(mask_f, axis=1, keepdims=True), (8, 128))

    pl.semaphore_wait(barrier, n - 1 + grps - 1)

    def kv_copy(g, s, target):
        return pltpu.make_async_remote_copy(
            src_ref=kvwin.at[g, :, halo], dst_ref=kvwin.at[g, :, halo - s],
            send_sem=kv_ss.at[g, s - 1], recv_sem=kv_rs.at[g, s - 1],
            device_id={"ctx": target}, device_id_type=MESH)

    def part_copy(g, s, target):
        return pltpu.make_async_remote_copy(
            src_ref=part_send.at[g, s - 1], dst_ref=part_recv.at[g, s - 1],
            send_sem=pt_ss.at[g, s - 1], recv_sem=pt_rs.at[g, s - 1],
            device_id={"ctx": target}, device_id_type=MESH)

    def dq_out(g, peer):
        return pltpu.make_async_remote_copy(
            src_ref=dq_send.at[g, peer], dst_ref=dq_recv.at[g, me],
            send_sem=dq_ss.at[g, peer], recv_sem=dq_rs.at[g, me],
            device_id={"ctx": peer}, device_id_type=MESH)

    def dq_in(g, peer):
        return pltpu.make_async_remote_copy(
            src_ref=dq_send.at[g, peer], dst_ref=dq_recv.at[g, peer],
            send_sem=dq_ss.at[g, peer], recv_sem=dq_rs.at[g, peer],
            device_id={"ctx": peer}, device_id_type=MESH)

    def count_copy(buffer, ss, rs, axis, own, slot, peer):
        return pltpu.make_async_remote_copy(
            src_ref=buffer.at[own], dst_ref=buffer.at[slot],
            send_sem=ss.at[peer], recv_sem=rs.at[slot],
            device_id={axis: peer}, device_id_type=MESH)

    for peer in peers:
        count_copy(cnt_ctx, c1_ss, c1_rs, "ctx", me, me, peer).start()
    for g in range(KVH):
        for copy in kv_copies[g]:
            copy.wait()
        for s in range(1, halo + 1):
            @pl.when(me + s < n)
            def _():
                kv_copy(g, s, me + s).start()

    plan_copy.wait()
    docs_copy.wait()
    plan_f = plan_ref[...].astype(jnp.float32)
    plan_b = jnp.broadcast_to(plan_f, (spans, spans))
    plan_t = jnp.transpose(plan_b)
    dest_b = jnp.floor(plan_b * (1.0 / per_device))
    dest_t = jnp.floor(plan_t * (1.0 / per_device))
    row_id = lax.broadcasted_iota(jnp.int32, (spans, spans), 0)
    col_id = lax.broadcasted_iota(jnp.int32, (spans, spans), 1)
    earlier = (dest_b == dest_t) & (row_id // per_device == col_id // per_device) & (col_id < row_id)
    rank_t = jnp.sum(jnp.where(earlier, 1.0, 0.0), axis=1, keepdims=True)
    span_id = lax.broadcasted_iota(jnp.int32, (spans, rows), 0)
    tok_id = lax.broadcasted_iota(jnp.int32, (spans, rows), 1)
    dest_c = dest_t[:, :1]
    plan_c = plan_t[:, :1]
    send_c = dest_c * float(pair_rows) + rank_t * float(SPAN)
    origin = (lax.broadcasted_iota(jnp.int32, (spans, 1), 0) // per_device).astype(jnp.float32)
    recv_c = origin * float(pair_rows) + rank_t * float(SPAN)
    tok = lax.broadcasted_iota(jnp.int32, (1, rows), 1)
    within = lax.rem(tok, SPAN).astype(jnp.float32)
    own_span = span_id == me * per_device + tok_id // SPAN
    send_row = jnp.sum(jnp.where(own_span, send_c, 0.0), axis=0, keepdims=True) + within
    slot_f = (me * per_device + tok_id // SPAN).astype(jnp.float32)
    recv_row = jnp.sum(jnp.where(plan_c == slot_f, recv_c, 0.0), axis=0, keepdims=True) + within
    buffer_id = lax.broadcasted_iota(jnp.int32, (n * pair_rows, rows), 0).astype(jnp.float32)
    pack = jnp.where(buffer_id == send_row, 1.0, 0.0).astype(jnp.bfloat16)
    unpack = jnp.transpose(jnp.where(buffer_id == recv_row, 1.0, 0.0)).astype(jnp.bfloat16)

    query_pos = me * rows + tok
    start = jnp.zeros_like(query_pos)
    end = jnp.int32(0)
    for m in range(docs_ref.shape[1]):
        end = end + docs_ref[0, m]
        start = jnp.where(query_pos >= end, end, start)
    key_pos = (me - halo) * rows + lax.broadcasted_iota(jnp.int32, (window, rows), 0)
    bias_ref[...] = jnp.where((key_pos >= start) & (key_pos <= query_pos), 0.0, NEGATIVE)
    mask_col = jnp.transpose(jnp.broadcast_to(mask_f, (HD, rows))).astype(jnp.bfloat16)

    for peer in peers:
        count_copy(cnt_ctx, c1_ss, c1_rs, "ctx", me, peer, peer).wait_recv()
    cnt_grp[my_grp] = jnp.sum(cnt_ctx[...], axis=0)
    for peer in grp_peers:
        count_copy(cnt_grp, c2_ss, c2_rs, "grp", my_grp, my_grp, peer).start()

    scale_value = HD ** (-0.5)
    exp_scale = scale_value * math.log2(math.e)
    ones = jnp.ones((8, 2 * HD), jnp.bfloat16)
    factor = None
    for g in range(KVH):
        for s in range(1, halo + 1):
            @pl.when(me >= s)
            def _():
                kv_copy(g, s, me).wait_recv()

            @pl.when(me < s)
            def _():
                kvwin[g, :, halo - s] = jnp.zeros((2, rows, HD), jnp.bfloat16)
        for copy in qog_copies[g]:
            copy.wait()
        keys = kvwin[g, 0].reshape(window, HD)
        values = kvwin[g, 1].reshape(window, HD)
        keys_t = jnp.transpose(keys)
        dk_sum = jnp.zeros((window, HD), jnp.float32)
        dv_sum = jnp.zeros((window, HD), jnp.float32)
        for pair in range(GROUP // 2):
            columns = [slice(h * HD, (h + 1) * HD) for h in (g * GROUP + 2 * pair, g * GROUP + 2 * pair + 1)]
            queries = jnp.concatenate([q_ref[:, c] for c in columns], axis=0)
            grads = jnp.concatenate([g_ref[:, c] * mask_col for c in columns], axis=0)
            outputs = jnp.concatenate([o_ref[:, c] for c in columns], axis=0)
            product = grads.astype(jnp.float32) * outputs.astype(jnp.float32)
            high = product.astype(jnp.bfloat16)
            low = (product - high.astype(jnp.float32)).astype(jnp.bfloat16)
            delta = dot(ones, jnp.concatenate([high, low], axis=1), 1, 1)[:1]
            bias = bias_ref[...]
            scores = dot(keys, queries, 1, 1) * exp_scale + jnp.concatenate([bias, bias], axis=1)
            weights = jnp.exp2(scores - jnp.max(scores, axis=0, keepdims=True))
            probs = weights * (1.0 / jnp.sum(weights, axis=0, keepdims=True))
            dprobs = dot(values, grads, 1, 1)
            dscores = (probs * (dprobs - delta) * scale_value).astype(jnp.bfloat16)
            dq_t = dot(keys_t, dscores, 1, 0)
            if factor is None:
                for peer in grp_peers:
                    count_copy(cnt_grp, c2_ss, c2_rs, "grp", my_grp, peer, peer).wait_recv()
                counted = jnp.sum(cnt_grp[...], axis=0)[:1, :]
                factor = float(grps * n * rows) / jnp.maximum(counted, 1.0)
            dq_half = (dq_t * factor[:, :1]).astype(jnp.bfloat16)
            for i in range(2):
                packed = dot(pack, dq_half[:, i * rows:(i + 1) * rows], 1, 1).astype(jnp.bfloat16)
                local = (2 * pair + i) * HD
                dq_send[g, :, :, local:local + HD] = packed.reshape(n, pair_rows, HD)
            dk_sum += dot(dscores, queries, 1, 0)
            dv_sum += dot(probs.astype(jnp.bfloat16), grads, 1, 0)
        for peer in peers:
            dq_out(g, peer).start()
        dq_recv[g, me] = dq_send[g, me]
        for s in range(1, halo + 1):
            at = slice((halo - s) * rows, (halo - s + 1) * rows)
            part_send[g, s - 1, 0] = dk_sum[at].astype(jnp.bfloat16)
            part_send[g, s - 1, 1] = dv_sum[at].astype(jnp.bfloat16)

            @pl.when(me >= s)
            def _():
                part_copy(g, s, me - s).start()
        part_own[g, 0] = dk_sum[halo * rows:]
        part_own[g, 1] = dv_sum[halo * rows:]

    for g in range(KVH):
        for s in range(1, halo + 1):
            @pl.when(me + s < n)
            def _():
                part_copy(g, s, me).wait_recv()

            @pl.when(me + s >= n)
            def _():
                part_recv[g, s - 1] = jnp.zeros((2, rows, HD), jnp.bfloat16)
        total = part_own[g]
        for s in range(1, halo + 1):
            total += part_recv[g, s - 1].astype(jnp.float32)
        total = (total * factor[:, :1]).astype(jnp.bfloat16)
        dk_ref[0, :, g * HD:(g + 1) * HD] = total[0]
        dv_ref[0, :, g * HD:(g + 1) * HD] = total[1]
        for peer in peers:
            dq_in(g, peer).wait_recv()
        dq_ref[0, :, g * width:(g + 1) * width] = dot(
            unpack, dq_recv[g].reshape(n * pair_rows, width), 1, 0).astype(jnp.bfloat16)

    for peer in peers:
        count_copy(cnt_ctx, c1_ss, c1_rs, "ctx", me, me, peer).wait_send()
    for peer in grp_peers:
        count_copy(cnt_grp, c2_ss, c2_rs, "grp", my_grp, my_grp, peer).wait_send()
    for g in range(KVH):
        for s in range(1, halo + 1):
            @pl.when(me + s < n)
            def _():
                kv_copy(g, s, me + s).wait_send()

            @pl.when(me >= s)
            def _():
                part_copy(g, s, me - s).wait_send()
        for peer in peers:
            dq_out(g, peer).wait_send()


def solution(mesh):
    n, grps = mesh.shape["ctx"], mesh.shape["grp"]

    def shards(*args):
        rows = args[0].shape[1]
        halo = min(n - 1, -(-(n * rows // 4 - 1) // rows))
        slot_count = -(-(rows // SPAN) // n)
        pair_rows = -(-slot_count * SPAN // 16) * 16
        vmem = pl.BlockSpec(memory_space=pltpu.VMEM)
        dma = pltpu.SemaphoreType.DMA
        bf16, f32 = jnp.bfloat16, jnp.float32
        return pl.pallas_call(
            functools.partial(kernel, n, grps, halo, pair_rows),
            out_shape=[
                jax.ShapeDtypeStruct((1, rows, QH * HD), bf16),
                jax.ShapeDtypeStruct((1, rows, KVH * HD), bf16),
                jax.ShapeDtypeStruct((1, rows, KVH * HD), bf16),
            ],
            in_specs=[pl.BlockSpec(memory_space=pltpu.HBM)] * 8,
            out_specs=[vmem] * 3,
            scratch_shapes=[
                pltpu.VMEM((KVH, 2, halo + 1, rows, HD), bf16),
                pltpu.VMEM((KVH, halo, 2, rows, HD), bf16),
                pltpu.VMEM((KVH, halo, 2, rows, HD), bf16),
                pltpu.VMEM((KVH, 2, rows, HD), f32),
                pltpu.VMEM((KVH, n, pair_rows, GROUP * HD), bf16),
                pltpu.VMEM((KVH, n, pair_rows, GROUP * HD), bf16),
                pltpu.VMEM((n, 8, 128), f32),
                pltpu.VMEM((grps, 8, 128), f32),
                pltpu.VMEM(((halo + 1) * rows, rows), f32),
                pltpu.VMEM((rows, QH * HD), bf16),
                pltpu.VMEM((rows, QH * HD), bf16),
                pltpu.VMEM((rows, QH * HD), bf16),
                pltpu.VMEM((1, rows), jnp.int32),
                pltpu.SMEM(args[6].shape, jnp.int32),
                pltpu.VMEM(args[7].shape, jnp.int32),
                dma((KVH, 2)), dma((KVH, 3)), dma((3,)),
                dma((KVH, halo)), dma((KVH, halo)),
                dma((KVH, halo)), dma((KVH, halo)),
                dma((KVH, n)), dma((KVH, n)),
                dma((n,)), dma((n,)), dma((grps,)), dma((grps,)),
            ],
            compiler_params=pltpu.CompilerParams(
                collective_id=0, has_side_effects=True, vmem_limit_bytes=60 * 1024 * 1024),
            cost_estimate=pl.CostEstimate(
                flops=10 * (halo + 1) * rows * rows * QH * HD, bytes_accessed=9 * rows * QH * HD,
                transcendentals=(halo + 1) * rows * rows * QH),
        )(*args)

    in_specs = (
        P("grp", "ctx", None),
        P("grp", "ctx", None),
        P("grp", "ctx", None),
        P("grp", "ctx", None),
        P("grp", "ctx", None),
        P("grp", "ctx"),
        P("grp", None),
        P("grp", None),
    )
    out_specs = (P("grp", "ctx", None), P("grp", "ctx", None), P("grp", "ctx", None))
    return jax.shard_map(shards, mesh=mesh, in_specs=in_specs, out_specs=out_specs, check_vma=False)
```

```python
import functools
import math

import jax
import jax.numpy as jnp
from jax import lax
from jax.experimental import pallas as pl
from jax.experimental.pallas import tpu as pltpu
from jax.sharding import PartitionSpec as P

HD = 128
QH = 32
KVH = 4
SPAN = 8
GROUP = QH // KVH
UNIT = 4
NEGATIVE = -1e30
MESH = pl.DeviceIdType.MESH


def dot(a, b, ca, cb):
    return lax.dot_general(a, b, (((ca,), (cb,)), ((), ())), preferred_element_type=jnp.float32)


def kernel(
    n, grps, halo, pair_rows,
    q_hbm, k_hbm, v_hbm, o_hbm, g_hbm, mask_hbm, docs_hbm, plan_hbm,
    dq_ref, dk_ref, dv_ref,
    kvwin, part_send, part_recv, part_own, dq_send, dq_recv, cnt_ctx, cnt_grp, bias_ref,
    q_ref, o_ref, g_ref, mask_ref, docs_ref, plan_ref, kv_in, qog_in, small_in,
    kv_ss, kv_rs, pt_ss, pt_rs, dq_ss, dq_rs, c1_ss, c1_rs, c2_ss, c2_rs,
):
    me = lax.axis_index("ctx")
    my_grp = lax.axis_index("grp")
    rows = q_ref.shape[0]
    spans = plan_ref.shape[1]
    per_device = rows // SPAN
    slots = halo + 1
    window = slots * rows
    width, load = UNIT * HD, GROUP * HD
    steps = sorted(range(1, n), key=lambda step: (abs(2 * step - n), step))
    peers = [lax.rem(me + step, n) for step in steps]
    grp_peers = [lax.rem(my_grp + step, grps) for step in range(1, grps)]

    def fetch(source, target, sem):
        copy = pltpu.make_async_copy(source, target, sem)
        copy.start()
        return copy

    mask_copy = fetch(mask_hbm, mask_ref, small_in.at[0])
    kv_copies = [
        [fetch(ref.at[0, :, g * HD:(g + 1) * HD], kvwin.at[g, i, halo], kv_in.at[g, i])
         for i, ref in enumerate((k_hbm, v_hbm))]
        for g in range(KVH)
    ]
    plan_copy = fetch(plan_hbm, plan_ref, small_in.at[1])
    docs_copy = fetch(docs_hbm, docs_ref, small_in.at[2])
    qog_copies = [
        [fetch(source.at[0, :, g * load:(g + 1) * load], target.at[:, g * load:(g + 1) * load], qog_in.at[g, i])
         for i, (source, target) in enumerate(((q_hbm, q_ref), (o_hbm, o_ref), (g_hbm, g_ref)))]
        for g in range(KVH)
    ]

    barrier = pltpu.get_barrier_semaphore()
    for peer in peers:
        pl.semaphore_signal(barrier, inc=1, device_id={"ctx": peer}, device_id_type=MESH)
    for peer in grp_peers:
        pl.semaphore_signal(barrier, inc=1, device_id={"grp": peer}, device_id_type=MESH)

    mask_copy.wait()
    mask_f = mask_ref[...].astype(jnp.float32)
    cnt_ctx[me] = jnp.broadcast_to(jnp.sum(mask_f, axis=1, keepdims=True), (8, 128))

    pl.semaphore_wait(barrier, n - 1 + grps - 1)

    def kv_copy(g, s, target):
        return pltpu.make_async_remote_copy(
            src_ref=kvwin.at[g, :, halo], dst_ref=kvwin.at[g, :, halo - s],
            send_sem=kv_ss.at[g, s - 1], recv_sem=kv_rs.at[g, s - 1],
            device_id={"ctx": target}, device_id_type=MESH)

    def part_copy(g, s, target):
        return pltpu.make_async_remote_copy(
            src_ref=part_send.at[g, s - 1], dst_ref=part_recv.at[g, s - 1],
            send_sem=pt_ss.at[g, s - 1], recv_sem=pt_rs.at[g, s - 1],
            device_id={"ctx": target}, device_id_type=MESH)

    def dq_out(g, peer):
        return pltpu.make_async_remote_copy(
            src_ref=dq_send.at[g, peer], dst_ref=dq_recv.at[g, me],
            send_sem=dq_ss.at[g, peer], recv_sem=dq_rs.at[g, me],
            device_id={"ctx": peer}, device_id_type=MESH)

    def dq_in(g, peer):
        return pltpu.make_async_remote_copy(
            src_ref=dq_send.at[g, peer], dst_ref=dq_recv.at[g, peer],
            send_sem=dq_ss.at[g, peer], recv_sem=dq_rs.at[g, peer],
            device_id={"ctx": peer}, device_id_type=MESH)

    def count_copy(buffer, ss, rs, axis, own, slot, peer):
        return pltpu.make_async_remote_copy(
            src_ref=buffer.at[own], dst_ref=buffer.at[slot],
            send_sem=ss.at[peer], recv_sem=rs.at[slot],
            device_id={axis: peer}, device_id_type=MESH)

    for peer in peers:
        count_copy(cnt_ctx, c1_ss, c1_rs, "ctx", me, me, peer).start()

    def send_keys(g):
        for copy in kv_copies[g]:
            copy.wait()
        for s in range(1, halo + 1):
            @pl.when(me + s < n)
            def _():
                kv_copy(g, s, me + s).start()

    send_keys(0)

    plan_copy.wait()
    docs_copy.wait()
    plan_f = plan_ref[...].astype(jnp.float32)
    plan_b = jnp.broadcast_to(plan_f, (spans, spans))
    plan_t = jnp.transpose(plan_b)
    dest_b = jnp.floor(plan_b * (1.0 / per_device))
    dest_t = jnp.floor(plan_t * (1.0 / per_device))
    row_id = lax.broadcasted_iota(jnp.int32, (spans, spans), 0)
    col_id = lax.broadcasted_iota(jnp.int32, (spans, spans), 1)
    earlier = (dest_b == dest_t) & (row_id // per_device == col_id // per_device) & (col_id < row_id)
    rank_t = jnp.sum(jnp.where(earlier, 1.0, 0.0), axis=1, keepdims=True)
    span_id = lax.broadcasted_iota(jnp.int32, (spans, rows), 0)
    tok_id = lax.broadcasted_iota(jnp.int32, (spans, rows), 1)
    dest_c = dest_t[:, :1]
    plan_c = plan_t[:, :1]
    send_c = dest_c * float(pair_rows) + rank_t * float(SPAN)
    origin = (lax.broadcasted_iota(jnp.int32, (spans, 1), 0) // per_device).astype(jnp.float32)
    recv_c = origin * float(pair_rows) + rank_t * float(SPAN)
    tok = lax.broadcasted_iota(jnp.int32, (1, rows), 1)
    within = lax.rem(tok, SPAN).astype(jnp.float32)
    own_span = span_id == me * per_device + tok_id // SPAN
    send_row = jnp.sum(jnp.where(own_span, send_c, 0.0), axis=0, keepdims=True) + within
    slot_f = (me * per_device + tok_id // SPAN).astype(jnp.float32)
    recv_row = jnp.sum(jnp.where(plan_c == slot_f, recv_c, 0.0), axis=0, keepdims=True) + within
    buffer_id = lax.broadcasted_iota(jnp.int32, (n * pair_rows, rows), 0).astype(jnp.float32)
    pack = jnp.where(buffer_id == send_row, 1.0, 0.0).astype(jnp.bfloat16)
    unpack = jnp.transpose(jnp.where(buffer_id == recv_row, 1.0, 0.0)).astype(jnp.bfloat16)

    query_pos = me * rows + tok
    start = jnp.zeros_like(query_pos)
    end = jnp.int32(0)
    for m in range(docs_ref.shape[1]):
        end = end + docs_ref[0, m]
        start = jnp.where(query_pos >= end, end, start)
    key_pos = (me - halo) * rows + lax.broadcasted_iota(jnp.int32, (window, rows), 0)
    bias_ref[...] = jnp.where((key_pos >= start) & (key_pos <= query_pos), 0.0, NEGATIVE)
    mask_col = jnp.transpose(jnp.broadcast_to(mask_f, (HD, rows))).astype(jnp.bfloat16)

    for peer in peers:
        count_copy(cnt_ctx, c1_ss, c1_rs, "ctx", me, peer, peer).wait_recv()
    cnt_grp[my_grp] = jnp.sum(cnt_ctx[...], axis=0)
    for peer in grp_peers:
        count_copy(cnt_grp, c2_ss, c2_rs, "grp", my_grp, my_grp, peer).start()

    scale_value = HD ** (-0.5)
    exp_scale = scale_value * math.log2(math.e)
    ones = jnp.ones((8, 2 * HD), jnp.bfloat16)
    factor = None
    for g in range(KVH):
        for s in range(1, halo + 1):
            @pl.when(me >= s)
            def _():
                kv_copy(g, s, me).wait_recv()

            @pl.when(me < s)
            def _():
                kvwin[g, :, halo - s] = jnp.zeros((2, rows, HD), jnp.bfloat16)
        if g + 1 < KVH:
            send_keys(g + 1)
        for copy in qog_copies[g]:
            copy.wait()
        keys = kvwin[g, 0].reshape(window, HD)
        values = kvwin[g, 1].reshape(window, HD)
        keys_t = jnp.transpose(keys)
        stacked = [[], [], [], []]
        for pair in range(GROUP // 2):
            columns = [slice(h * HD, (h + 1) * HD) for h in (g * GROUP + 2 * pair, g * GROUP + 2 * pair + 1)]
            queries = jnp.concatenate([q_ref[:, c] for c in columns], axis=0)
            grads = jnp.concatenate([g_ref[:, c] * mask_col for c in columns], axis=0)
            outputs = jnp.concatenate([o_ref[:, c] for c in columns], axis=0)
            product = grads.astype(jnp.float32) * outputs.astype(jnp.float32)
            high = product.astype(jnp.bfloat16)
            low = (product - high.astype(jnp.float32)).astype(jnp.bfloat16)
            delta = dot(ones, jnp.concatenate([high, low], axis=1), 1, 1)[:1]
            bias = bias_ref[...]
            scores = dot(keys, queries, 1, 1) * exp_scale + jnp.concatenate([bias, bias], axis=1)
            weights = jnp.exp2(scores - jnp.max(scores, axis=0, keepdims=True))
            probs = weights * (1.0 / jnp.sum(weights, axis=0, keepdims=True))
            dprobs = dot(values, grads, 1, 1)
            dscores = (probs * (dprobs - delta) * scale_value).astype(jnp.bfloat16)
            dq_t = dot(keys_t, dscores, 1, 0)
            if factor is None:
                for peer in grp_peers:
                    count_copy(cnt_grp, c2_ss, c2_rs, "grp", my_grp, peer, peer).wait_recv()
                counted = jnp.sum(cnt_grp[...], axis=0)[:1, :]
                factor = float(grps * n * rows) / jnp.maximum(counted, 1.0)
            dq_half = (dq_t * factor[:, :1]).astype(jnp.bfloat16)
            for i in range(2):
                packed = dot(pack, dq_half[:, i * rows:(i + 1) * rows], 1, 1).astype(jnp.bfloat16)
                unit, local = divmod(2 * pair + i, UNIT)
                unit += g * GROUP // UNIT
                dq_send[unit, :, :, local * HD:(local + 1) * HD] = packed.reshape(n, pair_rows, HD)
            if local == UNIT - 1:
                for peer in peers:
                    dq_out(unit, peer).start()
                dq_recv[unit, me] = dq_send[unit, me]
            for pieces, piece in zip(stacked, (dscores, queries, probs.astype(jnp.bfloat16), grads)):
                pieces.append(piece)
        all_ds, all_q, all_p, all_g = (jnp.concatenate(x, axis=a) for x, a in zip(stacked, (1, 0, 1, 0)))
        dk_sum = dot(all_ds, all_q, 1, 0)
        dv_sum = dot(all_p, all_g, 1, 0)
        for s in range(1, halo + 1):
            at = slice((halo - s) * rows, (halo - s + 1) * rows)
            part_send[g, s - 1, 0] = dk_sum[at].astype(jnp.bfloat16)
            part_send[g, s - 1, 1] = dv_sum[at].astype(jnp.bfloat16)

            @pl.when(me >= s)
            def _():
                part_copy(g, s, me - s).start()
        part_own[g, 0] = dk_sum[halo * rows:]
        part_own[g, 1] = dv_sum[halo * rows:]

    for g in range(KVH):
        for unit in range(g * GROUP // UNIT, (g + 1) * GROUP // UNIT):
            for peer in peers:
                dq_in(unit, peer).wait_recv()
            dq_ref[0, :, unit * width:(unit + 1) * width] = dot(
                unpack, dq_recv[unit].reshape(n * pair_rows, width), 1, 0).astype(jnp.bfloat16)
        for s in range(1, halo + 1):
            @pl.when(me + s < n)
            def _():
                part_copy(g, s, me).wait_recv()

            @pl.when(me + s >= n)
            def _():
                part_recv[g, s - 1] = jnp.zeros((2, rows, HD), jnp.bfloat16)
        total = part_own[g]
        for s in range(1, halo + 1):
            total += part_recv[g, s - 1].astype(jnp.float32)
        total = (total * factor[:, :1]).astype(jnp.bfloat16)
        dk_ref[0, :, g * HD:(g + 1) * HD] = total[0]
        dv_ref[0, :, g * HD:(g + 1) * HD] = total[1]

    for peer in peers:
        count_copy(cnt_ctx, c1_ss, c1_rs, "ctx", me, me, peer).wait_send()
    for peer in grp_peers:
        count_copy(cnt_grp, c2_ss, c2_rs, "grp", my_grp, my_grp, peer).wait_send()
    for g in range(KVH):
        for s in range(1, halo + 1):
            @pl.when(me + s < n)
            def _():
                kv_copy(g, s, me + s).wait_send()

            @pl.when(me >= s)
            def _():
                part_copy(g, s, me - s).wait_send()
    for unit in range(QH // UNIT):
        for peer in peers:
            dq_out(unit, peer).wait_send()


def solution(mesh):
    n, grps = mesh.shape["ctx"], mesh.shape["grp"]

    def shards(*args):
        rows = args[0].shape[1]
        halo = min(n - 1, -(-(n * rows // 4 - 1) // rows))
        slot_count = -(-(rows // SPAN) // n)
        pair_rows = -(-slot_count * SPAN // 16) * 16
        vmem = pl.BlockSpec(memory_space=pltpu.VMEM)
        dma = pltpu.SemaphoreType.DMA
        bf16, f32 = jnp.bfloat16, jnp.float32
        return pl.pallas_call(
            functools.partial(kernel, n, grps, halo, pair_rows),
            out_shape=[
                jax.ShapeDtypeStruct((1, rows, QH * HD), bf16),
                jax.ShapeDtypeStruct((1, rows, KVH * HD), bf16),
                jax.ShapeDtypeStruct((1, rows, KVH * HD), bf16),
            ],
            in_specs=[pl.BlockSpec(memory_space=pltpu.HBM)] * 8,
            out_specs=[vmem] * 3,
            scratch_shapes=[
                pltpu.VMEM((KVH, 2, halo + 1, rows, HD), bf16),
                pltpu.VMEM((KVH, halo, 2, rows, HD), bf16),
                pltpu.VMEM((KVH, halo, 2, rows, HD), bf16),
                pltpu.VMEM((KVH, 2, rows, HD), f32),
                pltpu.VMEM((QH // UNIT, n, pair_rows, UNIT * HD), bf16),
                pltpu.VMEM((QH // UNIT, n, pair_rows, UNIT * HD), bf16),
                pltpu.VMEM((n, 8, 128), f32),
                pltpu.VMEM((grps, 8, 128), f32),
                pltpu.VMEM(((halo + 1) * rows, rows), f32),
                pltpu.VMEM((rows, QH * HD), bf16),
                pltpu.VMEM((rows, QH * HD), bf16),
                pltpu.VMEM((rows, QH * HD), bf16),
                pltpu.VMEM((1, rows), jnp.int32),
                pltpu.SMEM(args[6].shape, jnp.int32),
                pltpu.VMEM(args[7].shape, jnp.int32),
                dma((KVH, 2)), dma((KVH, 3)), dma((3,)),
                dma((KVH, halo)), dma((KVH, halo)),
                dma((KVH, halo)), dma((KVH, halo)),
                dma((QH // UNIT, n)), dma((QH // UNIT, n)),
                dma((n,)), dma((n,)), dma((grps,)), dma((grps,)),
            ],
            compiler_params=pltpu.CompilerParams(
                collective_id=0, has_side_effects=True, vmem_limit_bytes=40 * 1024 * 1024),
            cost_estimate=pl.CostEstimate(
                flops=10 * (halo + 1) * rows * rows * QH * HD, bytes_accessed=9 * rows * QH * HD,
                transcendentals=(halo + 1) * rows * rows * QH),
        )(*[pltpu.with_memory_space_constraint(a, pltpu.HBM) for a in args])

    in_specs = (
        P("grp", "ctx", None),
        P("grp", "ctx", None),
        P("grp", "ctx", None),
        P("grp", "ctx", None),
        P("grp", "ctx", None),
        P("grp", "ctx"),
        P("grp", None),
        P("grp", None),
    )
    out_specs = (P("grp", "ctx", None), P("grp", "ctx", None), P("grp", "ctx", None))
    return jax.shard_map(shards, mesh=mesh, in_specs=in_specs, out_specs=out_specs, check_vma=False)
```

```python
import functools
import math

import jax
import jax.numpy as jnp
from jax import lax
from jax.experimental import pallas as pl
from jax.experimental.pallas import tpu as pltpu
from jax.sharding import PartitionSpec as P

HD = 128
QH = 32
KVH = 4
SPAN = 8
GROUP = QH // KVH
UNIT = 2
NEGATIVE = -1e30
MESH = pl.DeviceIdType.MESH


def dot(a, b, ca, cb):
    return lax.dot_general(a, b, (((ca,), (cb,)), ((), ())), preferred_element_type=jnp.float32)


def kernel(
    n, grps, halo, pair_rows,
    q_hbm, k_hbm, v_hbm, o_hbm, g_hbm, mask_hbm, docs_hbm, plan_hbm,
    dq_ref, dk_ref, dv_ref,
    kvwin, part_send, part_recv, part_own, dq_send, dq_recv, cnt_ctx, cnt_grp, bias_ref,
    q_ref, o_ref, g_ref, mask_ref, docs_ref, plan_ref, kv_in, qog_in, small_in,
    kv_ss, kv_rs, pt_ss, pt_rs, dq_ss, dq_rs, c1_ss, c1_rs, c2_ss, c2_rs,
):
    me = lax.axis_index("ctx")
    my_grp = lax.axis_index("grp")
    rows = q_ref.shape[0]
    spans = plan_ref.shape[1]
    per_device = rows // SPAN
    slots = halo + 1
    window = slots * rows
    width, load = UNIT * HD, GROUP * HD
    steps = sorted(range(1, n), key=lambda step: (abs(2 * step - n), step))
    peers = [lax.rem(me + step, n) for step in steps]
    grp_peers = [lax.rem(my_grp + step, grps) for step in range(1, grps)]

    def fetch(source, target, sem):
        copy = pltpu.make_async_copy(source, target, sem)
        copy.start()
        return copy

    mask_copy = fetch(mask_hbm, mask_ref, small_in.at[0])
    kv_copies = [
        [fetch(ref.at[0, :, g * HD:(g + 1) * HD], kvwin.at[g, i, halo], kv_in.at[g, i])
         for i, ref in enumerate((k_hbm, v_hbm))]
        for g in range(KVH)
    ]
    plan_copy = fetch(plan_hbm, plan_ref, small_in.at[1])
    docs_copy = fetch(docs_hbm, docs_ref, small_in.at[2])
    qog_copies = [
        [fetch(source.at[0, :, g * load:(g + 1) * load], target.at[:, g * load:(g + 1) * load], qog_in.at[g, i])
         for i, (source, target) in enumerate(((q_hbm, q_ref), (o_hbm, o_ref), (g_hbm, g_ref)))]
        for g in range(KVH)
    ]

    barrier = pltpu.get_barrier_semaphore()
    for peer in peers:
        pl.semaphore_signal(barrier, inc=1, device_id={"ctx": peer}, device_id_type=MESH)
    for peer in grp_peers:
        pl.semaphore_signal(barrier, inc=1, device_id={"grp": peer}, device_id_type=MESH)

    mask_copy.wait()
    mask_f = mask_ref[...].astype(jnp.float32)
    cnt_ctx[me] = jnp.broadcast_to(jnp.sum(mask_f, axis=1, keepdims=True), (8, 128))

    pl.semaphore_wait(barrier, n - 1 + grps - 1)

    def kv_copy(g, s, target):
        return pltpu.make_async_remote_copy(
            src_ref=kvwin.at[g, :, halo], dst_ref=kvwin.at[g, :, halo - s],
            send_sem=kv_ss.at[g, s - 1], recv_sem=kv_rs.at[g, s - 1],
            device_id={"ctx": target}, device_id_type=MESH)

    def part_copy(g, s, target):
        return pltpu.make_async_remote_copy(
            src_ref=part_send.at[g, s - 1], dst_ref=part_recv.at[g, s - 1],
            send_sem=pt_ss.at[g, s - 1], recv_sem=pt_rs.at[g, s - 1],
            device_id={"ctx": target}, device_id_type=MESH)

    def dq_out(g, peer):
        return pltpu.make_async_remote_copy(
            src_ref=dq_send.at[g, peer], dst_ref=dq_recv.at[g, me],
            send_sem=dq_ss.at[g, peer], recv_sem=dq_rs.at[g, me],
            device_id={"ctx": peer}, device_id_type=MESH)

    def dq_in(g, peer):
        return pltpu.make_async_remote_copy(
            src_ref=dq_send.at[g, peer], dst_ref=dq_recv.at[g, peer],
            send_sem=dq_ss.at[g, peer], recv_sem=dq_rs.at[g, peer],
            device_id={"ctx": peer}, device_id_type=MESH)

    def count_copy(buffer, ss, rs, axis, own, slot, peer):
        return pltpu.make_async_remote_copy(
            src_ref=buffer.at[own], dst_ref=buffer.at[slot],
            send_sem=ss.at[peer], recv_sem=rs.at[slot],
            device_id={axis: peer}, device_id_type=MESH)

    for peer in peers:
        count_copy(cnt_ctx, c1_ss, c1_rs, "ctx", me, me, peer).start()

    def send_keys(g):
        for copy in kv_copies[g]:
            copy.wait()
        for s in range(1, halo + 1):
            @pl.when(me + s < n)
            def _():
                kv_copy(g, s, me + s).start()

    send_keys(0)

    plan_copy.wait()
    docs_copy.wait()
    plan_f = plan_ref[...].astype(jnp.float32)
    plan_b = jnp.broadcast_to(plan_f, (spans, spans))
    plan_t = jnp.transpose(plan_b)
    dest_b = jnp.floor(plan_b * (1.0 / per_device))
    dest_t = jnp.floor(plan_t * (1.0 / per_device))
    row_id = lax.broadcasted_iota(jnp.int32, (spans, spans), 0)
    col_id = lax.broadcasted_iota(jnp.int32, (spans, spans), 1)
    earlier = (dest_b == dest_t) & (row_id // per_device == col_id // per_device) & (col_id < row_id)
    rank_t = jnp.sum(jnp.where(earlier, 1.0, 0.0), axis=1, keepdims=True)
    span_id = lax.broadcasted_iota(jnp.int32, (spans, rows), 0)
    tok_id = lax.broadcasted_iota(jnp.int32, (spans, rows), 1)
    dest_c = dest_t[:, :1]
    plan_c = plan_t[:, :1]
    send_c = dest_c * float(pair_rows) + rank_t * float(SPAN)
    origin = (lax.broadcasted_iota(jnp.int32, (spans, 1), 0) // per_device).astype(jnp.float32)
    recv_c = origin * float(pair_rows) + rank_t * float(SPAN)
    tok = lax.broadcasted_iota(jnp.int32, (1, rows), 1)
    within = lax.rem(tok, SPAN).astype(jnp.float32)
    own_span = span_id == me * per_device + tok_id // SPAN
    send_row = jnp.sum(jnp.where(own_span, send_c, 0.0), axis=0, keepdims=True) + within
    slot_f = (me * per_device + tok_id // SPAN).astype(jnp.float32)
    recv_row = jnp.sum(jnp.where(plan_c == slot_f, recv_c, 0.0), axis=0, keepdims=True) + within
    buffer_id = lax.broadcasted_iota(jnp.int32, (n * pair_rows, rows), 0).astype(jnp.float32)
    pack = jnp.where(buffer_id == send_row, 1.0, 0.0).astype(jnp.bfloat16)
    unpack = jnp.transpose(jnp.where(buffer_id == recv_row, 1.0, 0.0)).astype(jnp.bfloat16)

    query_pos = me * rows + tok
    start = jnp.zeros_like(query_pos)
    end = jnp.int32(0)
    for m in range(docs_ref.shape[1]):
        end = end + docs_ref[0, m]
        start = jnp.where(query_pos >= end, end, start)
    key_pos = (me - halo) * rows + lax.broadcasted_iota(jnp.int32, (window, rows), 0)
    bias_ref[...] = jnp.where((key_pos >= start) & (key_pos <= query_pos), 0.0, NEGATIVE)
    mask_col = jnp.transpose(jnp.broadcast_to(mask_f, (HD, rows))).astype(jnp.bfloat16)

    for peer in peers:
        count_copy(cnt_ctx, c1_ss, c1_rs, "ctx", me, peer, peer).wait_recv()
    cnt_grp[my_grp] = jnp.sum(cnt_ctx[...], axis=0)
    for peer in grp_peers:
        count_copy(cnt_grp, c2_ss, c2_rs, "grp", my_grp, my_grp, peer).start()

    scale_value = HD ** (-0.5)
    exp_scale = scale_value * math.log2(math.e)
    ones = jnp.ones((8, 2 * HD), jnp.bfloat16)
    factor = None
    for g in range(KVH):
        for s in range(1, halo + 1):
            @pl.when(me >= s)
            def _():
                kv_copy(g, s, me).wait_recv()

            @pl.when(me < s)
            def _():
                kvwin[g, :, halo - s] = jnp.zeros((2, rows, HD), jnp.bfloat16)
        if g + 1 < KVH:
            send_keys(g + 1)
        for copy in qog_copies[g]:
            copy.wait()
        keys = kvwin[g, 0].reshape(window, HD)
        values = kvwin[g, 1].reshape(window, HD)
        keys_t = jnp.transpose(keys)
        stacked = [[], [], [], []]
        for pair in range(GROUP // 2):
            columns = [slice(h * HD, (h + 1) * HD) for h in (g * GROUP + 2 * pair, g * GROUP + 2 * pair + 1)]
            queries = jnp.concatenate([q_ref[:, c] for c in columns], axis=0)
            grads = jnp.concatenate([g_ref[:, c] * mask_col for c in columns], axis=0)
            outputs = jnp.concatenate([o_ref[:, c] for c in columns], axis=0)
            product = grads.astype(jnp.float32) * outputs.astype(jnp.float32)
            high = product.astype(jnp.bfloat16)
            low = (product - high.astype(jnp.float32)).astype(jnp.bfloat16)
            delta = dot(ones, jnp.concatenate([high, low], axis=1), 1, 1)[:1]
            bias = bias_ref[...]
            scores = dot(keys, queries, 1, 1) * exp_scale + jnp.concatenate([bias, bias], axis=1)
            weights = jnp.exp2(scores - jnp.max(scores, axis=0, keepdims=True))
            probs = weights * (1.0 / jnp.sum(weights, axis=0, keepdims=True))
            dprobs = dot(values, grads, 1, 1)
            dscores = (probs * (dprobs - delta) * scale_value).astype(jnp.bfloat16)
            dq_t = dot(keys_t, dscores, 1, 0)
            if factor is None:
                for peer in grp_peers:
                    count_copy(cnt_grp, c2_ss, c2_rs, "grp", my_grp, peer, peer).wait_recv()
                counted = jnp.sum(cnt_grp[...], axis=0)[:1, :]
                factor = float(grps * n * rows) / jnp.maximum(counted, 1.0)
            dq_half = (dq_t * factor[:, :1]).astype(jnp.bfloat16)
            for i in range(2):
                packed = dot(pack, dq_half[:, i * rows:(i + 1) * rows], 1, 1).astype(jnp.bfloat16)
                unit, local = divmod(2 * pair + i, UNIT)
                unit += g * GROUP // UNIT
                dq_send[unit, :, :, local * HD:(local + 1) * HD] = packed.reshape(n, pair_rows, HD)
            if local == UNIT - 1:
                for peer in peers:
                    dq_out(unit, peer).start()
                dq_recv[unit, me] = dq_send[unit, me]
            for pieces, piece in zip(stacked, (dscores, queries, probs.astype(jnp.bfloat16), grads)):
                pieces.append(piece)
        all_ds, all_q, all_p, all_g = (jnp.concatenate(x, axis=a) for x, a in zip(stacked, (1, 0, 1, 0)))
        dk_sum = dot(all_ds, all_q, 1, 0)
        dv_sum = dot(all_p, all_g, 1, 0)
        for s in range(1, halo + 1):
            at = slice((halo - s) * rows, (halo - s + 1) * rows)
            part_send[g, s - 1, 0] = dk_sum[at].astype(jnp.bfloat16)
            part_send[g, s - 1, 1] = dv_sum[at].astype(jnp.bfloat16)

            @pl.when(me >= s)
            def _():
                part_copy(g, s, me - s).start()
        part_own[g, 0] = dk_sum[halo * rows:]
        part_own[g, 1] = dv_sum[halo * rows:]

    for g in range(KVH):
        for unit in range(g * GROUP // UNIT, (g + 1) * GROUP // UNIT):
            for peer in peers:
                dq_in(unit, peer).wait_recv()
            dq_ref[0, :, unit * width:(unit + 1) * width] = dot(
                unpack, dq_recv[unit].reshape(n * pair_rows, width), 1, 0).astype(jnp.bfloat16)
        for s in range(1, halo + 1):
            @pl.when(me + s < n)
            def _():
                part_copy(g, s, me).wait_recv()

            @pl.when(me + s >= n)
            def _():
                part_recv[g, s - 1] = jnp.zeros((2, rows, HD), jnp.bfloat16)
        total = part_own[g]
        for s in range(1, halo + 1):
            total += part_recv[g, s - 1].astype(jnp.float32)
        total = (total * factor[:, :1]).astype(jnp.bfloat16)
        dk_ref[0, :, g * HD:(g + 1) * HD] = total[0]
        dv_ref[0, :, g * HD:(g + 1) * HD] = total[1]

    for peer in peers:
        count_copy(cnt_ctx, c1_ss, c1_rs, "ctx", me, me, peer).wait_send()
    for peer in grp_peers:
        count_copy(cnt_grp, c2_ss, c2_rs, "grp", my_grp, my_grp, peer).wait_send()
    for g in range(KVH):
        for s in range(1, halo + 1):
            @pl.when(me + s < n)
            def _():
                kv_copy(g, s, me + s).wait_send()

            @pl.when(me >= s)
            def _():
                part_copy(g, s, me - s).wait_send()
    for unit in range(QH // UNIT):
        for peer in peers:
            dq_out(unit, peer).wait_send()


def solution(mesh):
    n, grps = mesh.shape["ctx"], mesh.shape["grp"]

    def shards(*args):
        rows = args[0].shape[1]
        halo = min(n - 1, -(-(n * rows // 4 - 1) // rows))
        slot_count = -(-(rows // SPAN) // n)
        pair_rows = -(-slot_count * SPAN // 16) * 16
        vmem = pl.BlockSpec(memory_space=pltpu.VMEM)
        dma = pltpu.SemaphoreType.DMA
        bf16, f32 = jnp.bfloat16, jnp.float32
        return pl.pallas_call(
            functools.partial(kernel, n, grps, halo, pair_rows),
            out_shape=[
                jax.ShapeDtypeStruct((1, rows, QH * HD), bf16),
                jax.ShapeDtypeStruct((1, rows, KVH * HD), bf16),
                jax.ShapeDtypeStruct((1, rows, KVH * HD), bf16),
            ],
            in_specs=[pl.BlockSpec(memory_space=pltpu.HBM)] * 8,
            out_specs=[vmem] * 3,
            scratch_shapes=[
                pltpu.VMEM((KVH, 2, halo + 1, rows, HD), bf16),
                pltpu.VMEM((KVH, halo, 2, rows, HD), bf16),
                pltpu.VMEM((KVH, halo, 2, rows, HD), bf16),
                pltpu.VMEM((KVH, 2, rows, HD), f32),
                pltpu.VMEM((QH // UNIT, n, pair_rows, UNIT * HD), bf16),
                pltpu.VMEM((QH // UNIT, n, pair_rows, UNIT * HD), bf16),
                pltpu.VMEM((n, 8, 128), f32),
                pltpu.VMEM((grps, 8, 128), f32),
                pltpu.VMEM(((halo + 1) * rows, rows), f32),
                pltpu.VMEM((rows, QH * HD), bf16),
                pltpu.VMEM((rows, QH * HD), bf16),
                pltpu.VMEM((rows, QH * HD), bf16),
                pltpu.VMEM((1, rows), jnp.int32),
                pltpu.SMEM(args[6].shape, jnp.int32),
                pltpu.VMEM(args[7].shape, jnp.int32),
                dma((KVH, 2)), dma((KVH, 3)), dma((3,)),
                dma((KVH, halo)), dma((KVH, halo)),
                dma((KVH, halo)), dma((KVH, halo)),
                dma((QH // UNIT, n)), dma((QH // UNIT, n)),
                dma((n,)), dma((n,)), dma((grps,)), dma((grps,)),
            ],
            compiler_params=pltpu.CompilerParams(
                collective_id=0, has_side_effects=True, vmem_limit_bytes=40 * 1024 * 1024),
            cost_estimate=pl.CostEstimate(
                flops=10 * (halo + 1) * rows * rows * QH * HD, bytes_accessed=9 * rows * QH * HD,
                transcendentals=(halo + 1) * rows * rows * QH),
        )(*[pltpu.with_memory_space_constraint(a, pltpu.HBM) for a in args])

    in_specs = (
        P("grp", "ctx", None),
        P("grp", "ctx", None),
        P("grp", "ctx", None),
        P("grp", "ctx", None),
        P("grp", "ctx", None),
        P("grp", "ctx"),
        P("grp", None),
        P("grp", None),
    )
    out_specs = (P("grp", "ctx", None), P("grp", "ctx", None), P("grp", "ctx", None))
    return jax.shard_map(shards, mesh=mesh, in_specs=in_specs, out_specs=out_specs, check_vma=False)
```
